256 devices in a mesh: section: 16 (over z_lo, x, core), expert: 16 (over z_hi, y).
Axes of the slice: x: 4, y: 4, z: 8 (z_hi: 4, z_lo: 2; z = z_hi * 2 + z_lo), core: 2. Of those that a mesh axis runs over, the one named last changes fastest.
Arguments:
- hidden: bfloat16 [16, 16, 1024, 1024], P('section', 'expert'), may hold values from -6 to 6
- down_weight: bfloat16 [16, 16, 1024, 3584], P('section', 'expert'), may hold values from -0.1875 to 0.1875
- expert_ids: int32 [65536, 2], P(('section', 'expert')), may hold values from 0 to 15, all different within a row; in each aligned block of 256 rows (0 to 255, 256 to 511, ...) at most 64 rows name the same one
- route_gates: bfloat16 [65536, 2], P(('section', 'expert')), may hold values from 0.099609375 to 1
- residual: bfloat16 [65536, 3584], P(('section', 'expert')), may hold values from -6 to 6
Outputs:
- handoff: bfloat16 [65536, 3584], P(('section', 'expert'))
The draws below stay inside these ranges and needn't reach their ends.
Inputs may be any that keep to these rules, and one draw needn't show every extreme that they name: `expert_ids`: each row names 2 different experts; in the rows of one device no expert is named by more than 64 rows, a bound that some block reaches.
All inputs are finite; a program needn't handle non-finite values.
Results may differ from the reference program's by a relative error of at most 0.0048.
Values may be sent and summed in bfloat16 or wider, within the bound.
A program may use at most 128 MiB of HBM per device.

```python
import math
import jax
import jax.numpy as jnp
import numpy as np
from jax import lax

D_WIN = 3584
FF = 1024
TOPK = 2
TOK_DEV = 256
EXPERTS = 16
CAP = 64
SLOTS = 1024
TOKENS = 65536
N_SECTION = 16
N_EXPERT = 16


def shard_levels(own_key, dims, cuts, low, top_value):
    level, own = 1.0, jax.random.fold_in(own_key, 6)
    for dim, parts in cuts:
        draws = jnp.exp(jax.random.uniform(jax.random.fold_in(own, dim), (parts,), jnp.float32, low / len(cuts), top_value / len(cuts)))
        level = level * jnp.repeat(draws, dims[dim] // parts).reshape([-1 if axis == dim else 1 for axis in range(len(dims))])
    return level


def shared_out(rng, own, number, rows, count, top, most, lean):
    order = jax.random.permutation(rng, count)
    packed, common = load_shares(count, rows * top, most, lean, True), load_shares(count, rows * top, most, lean, False)
    places = jnp.arange(count)

    def named(tallies, rotation):
        used = int((tallies > 0).sum())
        fixed = max(1, used // 4)
        moved = fixed + (places - fixed + rotation * (used - fixed)) % max(1, count - fixed)
        return jnp.zeros((count,), jnp.int32).at[order[jnp.where(places < fixed, places, moved)]].set(jnp.asarray(tallies, jnp.int32))

    tallies = jnp.where(number % 4 == 0, named(packed, number // 4), named(common, number - number // 4 - 1))
    mixed = jax.random.permutation(jax.random.fold_in(own, 3), count)
    donor, sink = mixed[0:count // 2 * 2:2], mixed[1:count // 2 * 2:2]
    margin = jnp.minimum(tallies[donor] - 1, most - tallies[sink]) // 2
    margin = jnp.where((donor == order[0]) | (sink == order[0]) | (tallies[sink] == 0), 0, jnp.maximum(margin, 0))
    moved = jax.random.randint(jax.random.fold_in(own, 4), (count // 2,), 0, 1 << 20) % (margin + 1)
    tallies = tallies.at[donor].add(-moved).at[sink].add(moved)
    members = jnp.searchsorted(jnp.cumsum(tallies), jnp.arange(rows * top), side="right").astype(jnp.int32)
    grid = members.reshape(top, rows).T
    grid = grid[jax.random.permutation(jax.random.fold_in(own, 1), rows)]
    rotation = jax.random.randint(jax.random.fold_in(own, 2), (rows, 1), 0, top)
    return jnp.take_along_axis(grid, (jnp.arange(top)[None, :] + rotation) % top, axis=1)


def load_shares(count, total, bound, slope, full):
    portions = [(1 << 20) // math.isqrt(grade ** slope) + 1 for grade in range(1, count + 1)]
    largest = bound if full else min(bound, max(-(-total // count), total * portions[0] // sum(portions)))
    least = 1 if total - largest >= count - 1 else 0
    holding, surplus = [largest] + [least] * (count - 1), total - largest - least * (count - 1)
    while surplus > 0:
        movable = [i for i in range(1, count) if holding[i] < largest] or [i for i in range(1, count) if holding[i] < bound]
        pool, budget = sum([portions[i] for i in movable]), surplus
        for i in movable:
            extra = min(bound - holding[i], max(1, budget * portions[i] // pool), surplus)
            holding[i] = holding[i] + extra
            surplus = surplus - extra
    return np.array(holding)


def noise(own_key, extent, scale, limit, split=(), held_as=jnp.bfloat16):
    array = scale * jax.random.normal(own_key, extent, jnp.float32)
    if split:
        array = array * shard_levels(own_key, extent, split, -0.22, 0.18)
    return jnp.clip(array, -limit, limit).astype(held_as)


def setup_inputs(seed: int = 0) -> dict:
    keys = jax.random.split(jax.random.key(seed), 6)
    hidden = noise(keys[0], (N_SECTION, EXPERTS, SLOTS, FF), 1.0, 6.0, ((0, 16), (1, 16)))
    down_weight = noise(keys[1], (N_SECTION, EXPERTS, FF, D_WIN), FF ** -0.5, 0.1875, ((0, 16), (1, 16)))
    expert_ids_keys = jax.random.split(jax.random.fold_in(keys[2], 1), TOKENS // TOK_DEV)
    expert_ids_turns = jax.random.permutation(jax.random.fold_in(keys[2], 3), TOKENS // TOK_DEV)
    expert_ids = jax.vmap(lambda own, number: shared_out(jax.random.fold_in(keys[2], 2), own, number, TOK_DEV, EXPERTS, TOPK, CAP, 2))(expert_ids_keys, expert_ids_turns).reshape((TOKENS, TOPK))
    route_gates = jnp.clip(0.099609375 + 0.9003906 * jax.random.uniform(keys[3], (TOKENS, TOPK), jnp.float32) ** shard_levels(keys[3], (TOKENS, TOPK), ((0, 256),), -0.2, 0.2), 0.099609375, 1.0).astype(jnp.bfloat16)
    residual = noise(keys[4], (TOKENS, D_WIN), 1.0, 6.0, ((0, 256),))
    return {"hidden": hidden, "down_weight": down_weight, "expert_ids": expert_ids, "route_gates": route_gates, "residual": residual}


def positions(route_ids):
    flat_ids = route_ids.reshape(-1)
    expert_cols = jnp.arange(EXPERTS, dtype=jnp.int32)
    onehot = (flat_ids[:, None] == expert_cols[None, :]).astype(jnp.int32)
    before = jnp.cumsum(onehot, axis=0) - onehot
    position = jnp.sum(before * onehot, axis=1)
    return position.reshape(route_ids.shape).astype(jnp.int32)


def project(pair_args):
    return jnp.dot(pair_args[0], pair_args[1], preferred_element_type=jnp.float32).astype(jnp.bfloat16)


def one_section(section_args):
    hidden_s, weight_s, section_ids, section_gates, section_rows = section_args
    outputs = lax.map(project, (hidden_s, weight_s))
    position = jax.vmap(positions)(section_ids)
    source = jnp.arange(N_EXPERT, dtype=jnp.int32)[:, None, None]
    slot_index = (source * CAP + position).astype(jnp.int32)
    picked = outputs[section_ids, slot_index]
    branch = jnp.sum(section_gates.astype(jnp.float32)[..., None] * picked.astype(jnp.float32), axis=2)
    branch = lax.optimization_barrier(branch.astype(jnp.bfloat16))
    return (section_rows.astype(jnp.float32) + branch.astype(jnp.float32)).astype(jnp.bfloat16)


def reference(hidden, down_weight, expert_ids, route_gates, residual):
    section_ids = expert_ids.reshape(N_SECTION, N_EXPERT, TOK_DEV, TOPK)
    section_gates = route_gates.reshape(N_SECTION, N_EXPERT, TOK_DEV, TOPK)
    section_rows = residual.reshape(N_SECTION, N_EXPERT, TOK_DEV, D_WIN)
    layer_out = lax.map(one_section, (hidden, down_weight, section_ids, section_gates, section_rows))
    handoff = jnp.roll(layer_out, 1, axis=0)
    return handoff.reshape(TOKENS, D_WIN)
```

```python
import functools

import jax
import jax.numpy as jnp
from jax import lax
from jax.experimental import pallas as pl
from jax.experimental.pallas import tpu as pltpu
from jax.sharding import PartitionSpec as P

MESH = pl.DeviceIdType.MESH
SIDE = 4
CHUNK = 256
HALF = CHUNK // 2
UP, DOWN = 0, 1


def kernel(
    sections, chunks, cap,
    hidden_hbm, weight_hbm, ids_ref, gates_ref, residual_hbm,
    out_hbm,
    hidden, weight, residual, ysend, yrecv, far_send, far_recv, near_send, near_recv, layer,
    table, mixing,
    hidden_sem, weight_sem, residual_sem, table_send, table_recv,
    y_ssem, y_rsem, far_ssem, far_rsem, near_ssem, near_rsem, hand_ssem, hand_rsem,
):
    s, e = lax.axis_index("section"), lax.axis_index("expert")
    z, y = e // SIDE, e % SIDE
    group = SIDE * cap
    rows = ids_ref.shape[1]

    def at_y(step):
        return (s, z * SIDE + (y + step) % SIDE)

    def at_z(step):
        return (s, ((z + step) % SIDE) * SIDE + y)

    following = ((s + 1) % sections, e)
    preceding = ((s + sections - 1) % sections, e)

    barrier = pltpu.get_barrier_semaphore()
    partners = [at_y(1), at_y(2), at_y(3), at_z(1), at_z(2), at_z(3), preceding]
    for partner in partners:
        pl.semaphore_signal(barrier, inc=1, device_id=partner, device_id_type=MESH)

    def columns(c):
        return pl.ds(pl.multiple_of(c * CHUNK, CHUNK), CHUNK)

    def load_weight(c):
        return pltpu.make_async_copy(weight_hbm.at[0, 0, :, columns(c)], weight.at[c], weight_sem.at[c])

    def load_residual(c):
        return pltpu.make_async_copy(residual_hbm.at[:, columns(c)], residual.at[c], residual_sem.at[c])

    load_hidden = pltpu.make_async_copy(hidden_hbm.at[0, 0], hidden, hidden_sem)
    load_hidden.start()

    @pl.loop(0, chunks)
    def _(c):
        load_weight(c).start()

    @pl.loop(0, chunks)
    def _(c):
        load_residual(c).start()

    ids = ids_ref[...]
    experts = lax.broadcasted_iota(jnp.int32, (SIDE * SIDE, rows), 0)
    named = [(experts == ids[k:k + 1]).astype(jnp.float32) for k in range(2)]
    earlier = (lax.broadcasted_iota(jnp.int32, (rows, rows), 0) < lax.broadcasted_iota(jnp.int32, (rows, rows), 1))
    before = jnp.dot(
        (named[0] + named[1]).astype(jnp.bfloat16), earlier.astype(jnp.bfloat16), preferred_element_type=jnp.float32
    )
    slots = [
        ids[k:k + 1].astype(jnp.float32) * cap + jnp.sum(before * named[k], axis=0, keepdims=True) for k in range(2)
    ]
    gates = gates_ref[...].astype(jnp.float32)
    table[z] = jnp.concatenate([slots[0], slots[1], gates, jnp.zeros((4, rows), jnp.float32)], axis=0)

    def produce(c):
        load_weight(c).wait()
        for zd in range(SIDE):
            block = jnp.dot(
                hidden[zd * group:(zd + 1) * group], weight[c], preferred_element_type=jnp.float32
            ).astype(jnp.bfloat16)
            ysend[c, :, zd] = block.reshape(SIDE, cap, CHUNK)
        yrecv[c, :, y] = ysend[c, y]

    def y_copy(c, step):
        yd = (y + step) % SIDE
        return pltpu.make_async_remote_copy(
            src_ref=ysend.at[c, yd], dst_ref=yrecv.at[c, :, y],
            send_sem=y_ssem.at[c, step - 1], recv_sem=y_rsem.at[c, step - 1],
            device_id=at_y(step), device_id_type=MESH,
        )

    def table_copy(step):
        return pltpu.make_async_remote_copy(
            src_ref=table.at[z], dst_ref=table.at[z],
            send_sem=table_send.at[step - 1], recv_sem=table_recv.at[step - 1],
            device_id=at_z(step), device_id_type=MESH,
        )

    def far_copy(c, way):
        return pltpu.make_async_remote_copy(
            src_ref=far_send.at[c, way], dst_ref=far_recv.at[c, way],
            send_sem=far_ssem.at[c, way], recv_sem=far_rsem.at[c, way],
            device_id=at_z(1 if way == UP else 3), device_id_type=MESH,
        )

    def near_copy(c, way, part):
        return pltpu.make_async_remote_copy(
            src_ref=near_send.at[c, way, part], dst_ref=near_recv.at[c, way, part],
            send_sem=near_ssem.at[c, way, part], recv_sem=near_rsem.at[c, way, part],
            device_id=at_z(1 if way == UP else 3), device_id_type=MESH,
        )

    def hand_copy(c):
        return pltpu.make_async_remote_copy(
            src_ref=layer.at[c], dst_ref=out_hbm.at[:, columns(c)],
            send_sem=hand_ssem.at[c], recv_sem=hand_rsem.at[c],
            device_id=following, device_id_type=MESH,
        )

    def partial(c, step, part):
        zd = (z + step) % SIDE
        mine = yrecv[c, zd].reshape(group, CHUNK)
        if part is not None:
            mine = mine[:, part * HALF:(part + 1) * HALF]
        return jnp.dot(mixing[zd], mine, preferred_element_type=jnp.float32)

    def scatter(c):
        for step in (1, 2, 3):
            y_copy(c, step).wait_recv()
        for way in (UP, DOWN):
            far_send[c, way] = partial(c, 2, 1 - way).astype(jnp.bfloat16)
            far_copy(c, way).start()
        for way in (UP, DOWN):
            near_send[c, way, way] = partial(c, 1 if way == UP else 3, way).astype(jnp.bfloat16)
            near_copy(c, way, way).start()

    def pass_on(c):
        for way in (UP, DOWN):
            own = partial(c, 1 if way == UP else 3, 1 - way)
            far_copy(c, way).wait_recv()
            near_send[c, way, 1 - way] = (own + far_recv[c, way].astype(jnp.float32)).astype(jnp.bfloat16)
            near_copy(c, way, 1 - way).start()

    def finish(c):
        own = partial(c, 0, None)
        for way in (UP, DOWN):
            for part in (0, 1):
                near_copy(c, way, part).wait_recv()
        load_residual(c).wait()
        for part in (0, 1):
            cols = slice(part * HALF, (part + 1) * HALF)
            branch = own[:, cols] + near_recv[c, UP, part].astype(jnp.float32) + near_recv[c, DOWN, part].astype(jnp.float32)
            branch = branch.astype(jnp.bfloat16).astype(jnp.float32)
            layer[c, :, cols] = (residual[c, :, cols].astype(jnp.float32) + branch).astype(jnp.bfloat16)
        hand_copy(c).start()

    def mix():
        for step in (1, 2, 3):
            table_copy(step).wait_recv()
        slot = lax.broadcasted_iota(jnp.int32, (group, rows), 0).astype(jnp.float32) + (z * group).astype(jnp.float32)
        for zd in range(SIDE):
            entry = table[zd]
            weights = jnp.where(slot == entry[0:1], entry[2:3], 0.0) + jnp.where(slot == entry[1:2], entry[3:4], 0.0)
            mixing[zd] = weights.T.astype(jnp.bfloat16)

    load_hidden.wait()
    produce(0)
    pl.semaphore_wait(barrier, len(partners))
    for step in (1, 2, 3):
        y_copy(0, step).start()
    for step in (1, 2, 3):
        table_copy(step).start()

    @pl.loop(0, chunks + 2)
    def _(i):
        @pl.when(i < chunks - 1)
        def _():
            produce(i + 1)
            for step in (1, 2, 3):
                y_copy(i + 1, step).start()

        @pl.when(i == 0)
        def _():
            mix()

        @pl.when(i < chunks)
        def _():
            scatter(i)

        @pl.when((i >= 1) & (i <= chunks))
        def _():
            pass_on(i - 1)

        @pl.when(i >= 2)
        def _():
            finish(i - 2)

    @pl.loop(0, chunks)
    def _(c):
        for step in (1, 2, 3):
            y_copy(c, step).wait_send()
        for way in (UP, DOWN):
            far_copy(c, way).wait_send()
            for part in (0, 1):
                near_copy(c, way, part).wait_send()
        hand_copy(c).wait()

    for step in (1, 2, 3):
        table_copy(step).wait_send()


def local(hidden, down_weight, expert_ids, route_gates, residual):
    sections = lax.axis_size("section")
    slots, depth = hidden.shape[2:]
    rows, width = residual.shape
    cap = slots // (SIDE * SIDE)
    chunks = width // CHUNK
    group = SIDE * cap
    bf16, f32 = jnp.bfloat16, jnp.float32
    anywhere = pl.BlockSpec(memory_space=pl.ANY)
    vmem = pl.BlockSpec(memory_space=pltpu.VMEM)
    dma = pltpu.SemaphoreType.DMA
    return pl.pallas_call(
        functools.partial(kernel, sections, chunks, cap),
        out_shape=jax.ShapeDtypeStruct((rows, width), bf16),
        in_specs=[anywhere, anywhere, vmem, vmem, anywhere],
        out_specs=anywhere,
        scratch_shapes=[
            pltpu.VMEM((slots, depth), bf16),
            pltpu.VMEM((chunks, depth, CHUNK), bf16),
            pltpu.VMEM((chunks, rows, CHUNK), bf16),
            pltpu.VMEM((chunks, SIDE, SIDE, cap, CHUNK), bf16),
            pltpu.VMEM((chunks, SIDE, SIDE, cap, CHUNK), bf16),
            pltpu.VMEM((chunks, 2, rows, HALF), bf16),
            pltpu.VMEM((chunks, 2, rows, HALF), bf16),
            pltpu.VMEM((chunks, 2, 2, rows, HALF), bf16),
            pltpu.VMEM((chunks, 2, 2, rows, HALF), bf16),
            pltpu.VMEM((chunks, rows, CHUNK), bf16),
            pltpu.VMEM((SIDE, 8, rows), f32),
            pltpu.VMEM((SIDE, rows, group), bf16),
            dma(()), dma((chunks,)), dma((chunks,)), dma((3,)), dma((3,)),
            dma((chunks, 3)), dma((chunks, 3)),
            dma((chunks, 2)), dma((chunks, 2)),
            dma((chunks, 2, 2)), dma((chunks, 2, 2)),
            dma((chunks,)), dma((chunks,)),
        ],
        compiler_params=pltpu.CompilerParams(
            collective_id=0, has_side_effects=True, vmem_limit_bytes=56 * 2**20
        ),
        cost_estimate=pl.CostEstimate(
            flops=2 * slots * width * (depth + rows), bytes_accessed=2 * (slots * depth + depth * width + 2 * rows * width),
            transcendentals=0,
        ),
        name="down_combine_handoff",
    )(hidden, down_weight, expert_ids.T, route_gates.T, residual)


def solution(mesh):
    return jax.shard_map(
        local,
        mesh=mesh,
        in_specs=(
            P("section", "expert", None, None),
            P("section", "expert", None, None),
            P(("section", "expert"), None),
            P(("section", "expert"), None),
            P(("section", "expert"), None),
        ),
        out_specs=P(("section", "expert"), None),
        check_vma=False,
    )
```

```python
import functools

import jax
import jax.numpy as jnp
from jax import lax
from jax.experimental import pallas as pl
from jax.experimental.pallas import tpu as pltpu
from jax.sharding import PartitionSpec as P

MESH = pl.DeviceIdType.MESH
SIDE = 4
RUN = 8
CHUNK = 256
IN_VMEM = True
READ = 4
AHEAD = 1
STEPS = (2, 1, 3, 0)
FAR, NEAR, OWN = slice(0, 1), slice(1, 3), slice(3, 4)
ALL = slice(0, 4)
UP, DOWN = 0, 1


def kernel(
    sections, chunks, cap,
    hidden_hbm, weight_hbm, ids_ref, gates_ref, residual_hbm,
    out_hbm,
    hidden, weight, residual, ysend, yrecv, far_send, far_recv, near_send, near_recv, twin_send, twin_recv, layer,
    table, mixing,
    hidden_sem, weight_sem, residual_sem, table_send, table_recv,
    y_ssem, y_rsem, far_ssem, far_rsem, near_ssem, near_rsem, twin_ssem, twin_rsem, hand_ssem, hand_rsem,
):
    s, e = lax.axis_index("section"), lax.axis_index("expert")
    z, y = e // SIDE, e % SIDE
    group = SIDE * cap
    rows = ids_ref.shape[1]
    half = rows // 2

    def at_y(step):
        return (s, z * SIDE + (y + step) % SIDE)

    def at_z(step, section=s):
        return (section, ((z + step) % SIDE) * SIDE + y)

    last = s % RUN == RUN - 1
    twin = (s + RUN) % sections
    lent = jnp.where(s < RUN, DOWN, UP)
    following = (jnp.where(last, (twin + 1) % sections, (s + 1) % sections), e)
    preceding = (jnp.where(s % RUN == 0, (s + RUN - 1) % sections, (s + sections - 1) % sections), e)
    lender = at_z(jnp.where(s < RUN, SIDE - 1, 1), twin)

    barrier = pltpu.get_barrier_semaphore()
    partners = [at_y(1), at_y(2), at_y(3), at_z(1), at_z(2), at_z(3), preceding]
    for partner in partners:
        pl.semaphore_signal(barrier, inc=1, device_id=partner, device_id_type=MESH)

    @pl.when(last)
    def _():
        for partner in (lender, (twin, e)):
            pl.semaphore_signal(barrier, inc=1, device_id=partner, device_id_type=MESH)

    def columns(c):
        return pl.ds(pl.multiple_of(c * CHUNK, CHUNK), CHUNK)

    def load_weight(c):
        return pltpu.make_async_copy(weight_hbm.at[0, 0, :, columns(c)], weight.at[c], weight_sem.at[c])

    def load_residual(c):
        return pltpu.make_async_copy(residual_hbm.at[:, columns(c)], residual.at[c], residual_sem.at[c])

    def load_hidden(place):
        block = pl.ds(pl.multiple_of(((z + STEPS[place]) % SIDE) * group, group), group)
        return pltpu.make_async_copy(hidden_hbm.at[0, 0, block], hidden.at[place], hidden_sem.at[place])

    load_hidden(0).start()
    load_weight(0).start()
    for place in (1, 2, 3):
        load_hidden(place).start()

    ids = ids_ref[...]
    experts = lax.broadcasted_iota(jnp.int32, (SIDE * SIDE, rows), 0)
    named = [(experts == ids[k:k + 1]).astype(jnp.float32) for k in range(2)]
    earlier = (lax.broadcasted_iota(jnp.int32, (rows, rows), 0) < lax.broadcasted_iota(jnp.int32, (rows, rows), 1))
    before = jnp.dot(
        (named[0] + named[1]).astype(jnp.bfloat16), earlier.astype(jnp.bfloat16), preferred_element_type=jnp.float32
    )
    slots = [
        ids[k:k + 1].astype(jnp.float32) * cap + jnp.sum(before * named[k], axis=0, keepdims=True) for k in range(2)
    ]
    gates = gates_ref[...].astype(jnp.float32)
    table[z] = jnp.concatenate([slots[0], slots[1], gates, jnp.zeros((4, rows), jnp.float32)], axis=0)

    def produce_block(c, place):
        block = jnp.dot(hidden[place], weight[c], preferred_element_type=jnp.float32).astype(jnp.bfloat16)
        ysend[c, :, place] = block.reshape(SIDE, cap, CHUNK)
        yrecv[c, place, y] = ysend[c, y, place]

    def produce(c):
        load_weight(c).wait()
        for place in range(SIDE):
            produce_block(c, place)

    def y_copy(c, step, part):
        yd = (y + step) % SIDE
        number = (FAR, NEAR, OWN, ALL).index(part) % 3
        return pltpu.make_async_remote_copy(
            src_ref=ysend.at[c, yd, part], dst_ref=yrecv.at[c, part, y],
            send_sem=y_ssem.at[c, step - 1, number], recv_sem=y_rsem.at[c, step - 1, number],
            device_id=at_y(step), device_id_type=MESH,
        )

    def y_start(c, *parts):
        for part in parts:
            for step in (1, 2, 3):
                y_copy(c, step, part).start()

    def y_wait(c, part):
        for step in (1, 2, 3):
            y_copy(c, step, part).wait_recv()

    def table_copy(step):
        return pltpu.make_async_remote_copy(
            src_ref=table.at[z], dst_ref=table.at[z],
            send_sem=table_send.at[step - 1], recv_sem=table_recv.at[step - 1],
            device_id=at_z(step), device_id_type=MESH,
        )

    def far_copy(c, way):
        return pltpu.make_async_remote_copy(
            src_ref=far_send.at[c, way], dst_ref=far_recv.at[c, way],
            send_sem=far_ssem.at[c, way], recv_sem=far_rsem.at[c, way],
            device_id=at_z(1 if way == UP else 3), device_id_type=MESH,
        )

    def near_copy(c, way, part):
        lend = last & (lent == way)
        slot = jnp.where(lend, 1 - way, way)
        return pltpu.make_async_remote_copy(
            src_ref=near_send.at[c, way, part], dst_ref=near_recv.at[c, slot, part],
            send_sem=near_ssem.at[c, way, part], recv_sem=near_rsem.at[c, slot, part],
            device_id=at_z(1 if way == UP else 3, jnp.where(lend, twin, s)), device_id_type=MESH,
        )

    def near_wait(c, way):
        for part in (0, 1):
            pltpu.make_async_remote_copy(
                src_ref=near_send.at[c, way, part], dst_ref=near_recv.at[c, way, part],
                send_sem=near_ssem.at[c, way, part], recv_sem=near_rsem.at[c, way, part],
                device_id=at_z(1), device_id_type=MESH,
            ).wait_recv()

    def twin_copy(c):
        return pltpu.make_async_remote_copy(
            src_ref=twin_send.at[c], dst_ref=twin_recv.at[c],
            send_sem=twin_ssem.at[c], recv_sem=twin_rsem.at[c],
            device_id=(twin, e), device_id_type=MESH,
        )

    def hand_copy(c):
        return pltpu.make_async_remote_copy(
            src_ref=layer.at[c], dst_ref=out_hbm.at[:, columns(c)],
            send_sem=hand_ssem.at[c], recv_sem=hand_rsem.at[c],
            device_id=following, device_id_type=MESH,
        )

    def part_rows(part):
        return slice(part * half, (part + 1) * half)

    def partial(c, step, part):
        place = STEPS.index(step)
        mine = yrecv[c, place].reshape(group, CHUNK)
        return jnp.dot(mixing[place, part_rows(part)], mine, preferred_element_type=jnp.float32)

    def send_far(c):
        for way in (UP, DOWN):
            far_send[c, way] = partial(c, 2, 1 - way).astype(jnp.bfloat16)
            far_copy(c, way).start()

    def send_near(c):
        for way in (UP, DOWN):
            near_send[c, way, way] = partial(c, 1 if way == UP else 3, way).astype(jnp.bfloat16)
            near_copy(c, way, way).start()

    def pass_on(c):
        for way in (UP, DOWN):
            own = partial(c, 1 if way == UP else 3, 1 - way)
            far_copy(c, way).wait_recv()
            near_send[c, way, 1 - way] = (own + far_recv[c, way].astype(jnp.float32)).astype(jnp.bfloat16)
            near_copy(c, way, 1 - way).start()

    def finish(c):
        load_residual(c).wait()

        @pl.when(jnp.logical_not(last))
        def _():
            own = [partial(c, 0, part) for part in (0, 1)]
            near_wait(c, UP)
            near_wait(c, DOWN)
            for part in (0, 1):
                branch = own[part] + near_recv[c, UP, part].astype(jnp.float32) + near_recv[c, DOWN, part].astype(jnp.float32)
                branch = branch.astype(jnp.bfloat16).astype(jnp.float32)
                kept = residual[c, part_rows(part)].astype(jnp.float32)
                layer[c, part_rows(part)] = (kept + branch).astype(jnp.bfloat16)
            hand_copy(c).start()

        for way, here in ((UP, s < RUN), (DOWN, s >= RUN)):
            @pl.when(last & here)
            def _():
                own = [partial(c, 0, part) for part in (0, 1)]
                near_wait(c, way)
                for part in (0, 1):
                    branch = own[part] + near_recv[c, way, part].astype(jnp.float32)
                    kept = residual[c, part_rows(part)].astype(jnp.float32)
                    twin_send[c, part_rows(part)] = (kept + branch).astype(jnp.bfloat16)
                twin_copy(c).start()

    def finish_twin(c):
        for way, here in ((DOWN, s < RUN), (UP, s >= RUN)):
            @pl.when(here)
            def _():
                twin_copy(c).wait_recv()
                near_wait(c, way)
                for part in (0, 1):
                    summed = twin_recv[c, part_rows(part)].astype(jnp.float32) + near_recv[c, way, part].astype(jnp.float32)
                    layer[c, part_rows(part)] = summed.astype(jnp.bfloat16)
        hand_copy(c).start()

    def mix(place):
        entry = table[(z + STEPS[place]) % SIDE]
        slot = lax.broadcasted_iota(jnp.int32, (group, rows), 0).astype(jnp.float32) + (z * group).astype(jnp.float32)
        weights = jnp.where(slot == entry[0:1], entry[2:3], 0.0) + jnp.where(slot == entry[1:2], entry[3:4], 0.0)
        mixing[place] = weights.T.astype(jnp.bfloat16)

    def sent(c, *parts):
        for part in parts:
            for step in (1, 2, 3):
                y_copy(c, step, part).wait_send()
        for way in (UP, DOWN):
            far_copy(c, way).wait_send()
            for part in (0, 1):
                near_copy(c, way, part).wait_send()

        @pl.when(last)
        def _():
            twin_copy(c).wait_send()

    load_hidden(0).wait()
    load_weight(0).wait()
    produce_block(0, 0)
    pl.semaphore_wait(barrier, len(partners) + jnp.where(last, 2, 0))
    for step in (1, 2, 3):
        table_copy(step).start()
    y_start(0, FAR)
    for c in range(1, READ):
        load_weight(c).start()
    for place in (1, 2, 3):
        load_hidden(place).wait()
        produce_block(0, place)
        if place == 2:
            y_start(0, NEAR)
    y_start(0, OWN)
    for step in (1, 2, 3):
        table_copy(step).wait_recv()
    mix(0)
    y_wait(0, FAR)
    send_far(0)
    produce(1)
    y_start(1, FAR, NEAR, OWN)
    mix(1)
    mix(2)
    y_wait(0, NEAR)
    send_near(0)
    mix(3)
    load_residual(0).start()
    load_residual(1).start()
    for c in range(2, AHEAD + 2):
        produce(c)
        if c <= AHEAD:
            y_start(c, ALL)
    y_wait(0, OWN)

    def turn(i):
        split = isinstance(i, int)

        @pl.when(i < chunks - AHEAD)
        def _():
            y_start(i + AHEAD, ALL)

        @pl.when(i <= chunks - READ)
        def _():
            load_weight(i + READ - 1).start()

        @pl.when(i < chunks - 1)
        def _():
            load_residual(i + 1).start()

        @pl.when(i < chunks)
        def _():
            y_wait(i, FAR if split else ALL)
            send_far(i)
            if split:
                y_wait(i, NEAR)
            send_near(i)

        @pl.when(i < chunks - AHEAD - 1)
        def _():
            produce(i + AHEAD + 1)

        @pl.when(i <= chunks)
        def _():
            pass_on(i - 1)

        if split:
            y_wait(i, OWN)
            return

        @pl.when(i < chunks + 2)
        def _():
            finish(i - 2)

        @pl.when(last & (i >= 3))
        def _():
            finish_twin(i - 3)

        @pl.when(i >= 6)
        def _():
            sent(i - 4, ALL)

        @pl.when(i >= 8)
        def _():
            hand_copy(i - 8).wait()

    turn(1)
    pl.loop(2, chunks + 3)(turn)

    sent(0, FAR, NEAR, OWN)
    sent(1, FAR, NEAR, OWN)
    sent(chunks - 1, ALL)

    @pl.loop(chunks - 5, chunks)
    def _(c):
        hand_copy(c).wait()

    for step in (1, 2, 3):
        table_copy(step).wait_send()


def local(hidden, down_weight, expert_ids, route_gates, residual):
    sections = lax.axis_size("section")
    slots, depth = hidden.shape[2:]
    rows, width = residual.shape
    cap = slots // (SIDE * SIDE)
    chunks = width // CHUNK
    group = SIDE * cap
    bf16, f32 = jnp.bfloat16, jnp.float32
    anywhere = pl.BlockSpec(memory_space=pl.ANY)
    in_hbm = pl.BlockSpec(memory_space=pltpu.HBM)
    vmem = pl.BlockSpec(memory_space=pltpu.VMEM)
    dma = pltpu.SemaphoreType.DMA
    return pl.pallas_call(
        functools.partial(kernel, sections, chunks, cap),
        out_shape=pltpu.VMEM((rows, width), bf16) if IN_VMEM else jax.ShapeDtypeStruct((rows, width), bf16),
        in_specs=[in_hbm, in_hbm, vmem, vmem, in_hbm],
        out_specs=vmem if IN_VMEM else anywhere,
        scratch_shapes=[
            pltpu.VMEM((SIDE, group, depth), bf16),
            pltpu.VMEM((chunks, depth, CHUNK), bf16),
            pltpu.VMEM((chunks, rows, CHUNK), bf16),
            pltpu.VMEM((chunks, SIDE, SIDE, cap, CHUNK), bf16),
            pltpu.VMEM((chunks, SIDE, SIDE, cap, CHUNK), bf16),
            pltpu.VMEM((chunks, 2, rows // 2, CHUNK), bf16),
            pltpu.VMEM((chunks, 2, rows // 2, CHUNK), bf16),
            pltpu.VMEM((chunks, 2, 2, rows // 2, CHUNK), bf16),
            pltpu.VMEM((chunks, 2, 2, rows // 2, CHUNK), bf16),
            pltpu.VMEM((chunks, rows, CHUNK), bf16),
            pltpu.VMEM((chunks, rows, CHUNK), bf16),
            pltpu.VMEM((chunks, rows, CHUNK), bf16),
            pltpu.VMEM((SIDE, 8, rows), f32),
            pltpu.VMEM((SIDE, rows, group), bf16),
            dma((SIDE,)), dma((chunks,)), dma((chunks,)), dma((3,)), dma((3,)),
            dma((chunks, 3, 3)), dma((chunks, 3, 3)),
            dma((chunks, 2)), dma((chunks, 2)),
            dma((chunks, 2, 2)), dma((chunks, 2, 2)),
            dma((chunks,)), dma((chunks,)),
            dma((chunks,)), dma((chunks,)),
        ],
        compiler_params=pltpu.CompilerParams(
            collective_id=0, has_side_effects=True, vmem_limit_bytes=(61 if IN_VMEM else 56) * 2**20
        ),
        cost_estimate=pl.CostEstimate(
            flops=2 * slots * width * (depth + rows), bytes_accessed=2 * (slots * depth + depth * width + 2 * rows * width),
            transcendentals=0,
        ),
        name="down_combine_handoff",
    )(hidden, down_weight, expert_ids.T, route_gates.T, residual)


def solution(mesh):
    return jax.shard_map(
        local,
        mesh=mesh,
        in_specs=(
            P("section", "expert", None, None),
            P("section", "expert", None, None),
            P(("section", "expert"), None),
            P(("section", "expert"), None),
            P(("section", "expert"), None),
        ),
        out_specs=P(("section", "expert"), None),
        check_vma=False,
    )
```

```python
import functools

import jax
import jax.numpy as jnp
from jax import lax
from jax.experimental import pallas as pl
from jax.experimental.pallas import tpu as pltpu
from jax.sharding import PartitionSpec as P

MESH = pl.DeviceIdType.MESH
SIDE = 4
RUN = 8
CHUNK = 256
READ = 5
SPLIT = 2
AHEAD = 1
STEPS = (2, 1, 3, 0)
FAR, NEAR, OWN = slice(0, 1), slice(1, 3), slice(3, 4)
ALL = slice(0, 4)
UP, DOWN = 0, 1


def kernel(
    sections, chunks, cap,
    hidden_hbm, weight_hbm, ids_ref, gates_ref, residual_hbm,
    out_ref,
    hidden, weight, residual, ysend, yrecv, far_send, far_recv, near_send, near_recv, twin_send, twin_recv, layer,
    table, mixing,
    hidden_sem, weight_sem, residual_sem, table_send, table_recv,
    y_ssem, first_rsem, y_rsem, far_ssem, far_rsem, near_ssem, near_rsem, twin_ssem, twin_rsem, hand_ssem, hand_rsem,
):
    s, e = lax.axis_index("section"), lax.axis_index("expert")
    z, y = e // SIDE, e % SIDE
    group = SIDE * cap
    rows = ids_ref.shape[1]
    half = rows // 2

    def at_y(step):
        return (s, z * SIDE + (y + step) % SIDE)

    def at_z(step, section=s):
        return (section, ((z + step) % SIDE) * SIDE + y)

    last = s % RUN == RUN - 1
    twin = (s + RUN) % sections
    lent = jnp.where(s < RUN, DOWN, UP)
    following = (jnp.where(last, (twin + 1) % sections, (s + 1) % sections), e)
    preceding = (jnp.where(s % RUN == 0, (s + RUN - 1) % sections, (s + sections - 1) % sections), e)
    lender = at_z(jnp.where(s < RUN, SIDE - 1, 1), twin)

    barrier = pltpu.get_barrier_semaphore()
    partners = [at_y(1), at_y(2), at_y(3), at_z(1), at_z(2), at_z(3), preceding]
    for partner in partners:
        pl.semaphore_signal(barrier, inc=1, device_id=partner, device_id_type=MESH)

    @pl.when(last)
    def _():
        for partner in (lender, (twin, e)):
            pl.semaphore_signal(barrier, inc=1, device_id=partner, device_id_type=MESH)

    def columns(c):
        return pl.ds(pl.multiple_of(c * CHUNK, CHUNK), CHUNK)

    def load_weight(c):
        return pltpu.make_async_copy(weight_hbm.at[0, 0, :, columns(c)], weight.at[c], weight_sem.at[c])

    load_residual = pltpu.make_async_copy(residual_hbm, residual, residual_sem)

    def drain(ref, sem):
        pltpu.make_async_copy(ref, ref, sem).wait()

    def load_hidden(place):
        block = pl.ds(pl.multiple_of(((z + STEPS[place]) % SIDE) * group, group), group)
        return pltpu.make_async_copy(hidden_hbm.at[0, 0, block], hidden.at[place], hidden_sem.at[place])

    load_hidden(0).start()
    load_weight(0).start()
    for place in (1, 2, 3):
        load_hidden(place).start()

    ids = ids_ref[...]
    experts = lax.broadcasted_iota(jnp.int32, (SIDE * SIDE, rows), 0)
    named = [(experts == ids[k:k + 1]).astype(jnp.float32) for k in range(2)]
    earlier = (lax.broadcasted_iota(jnp.int32, (rows, rows), 0) < lax.broadcasted_iota(jnp.int32, (rows, rows), 1))
    before = jnp.dot(
        (named[0] + named[1]).astype(jnp.bfloat16), earlier.astype(jnp.bfloat16), preferred_element_type=jnp.float32
    )
    slots = [
        ids[k:k + 1].astype(jnp.float32) * cap + jnp.sum(before * named[k], axis=0, keepdims=True) for k in range(2)
    ]
    gates = gates_ref[...].astype(jnp.float32)
    table[z] = jnp.concatenate([slots[0], slots[1], gates, jnp.zeros((4, rows), jnp.float32)], axis=0)

    def produce_block(c, place):
        block = jnp.dot(hidden[place], weight[c], preferred_element_type=jnp.float32).astype(jnp.bfloat16)
        ysend[c, :, place] = block.reshape(SIDE, cap, CHUNK)
        yrecv[c, place, y] = ysend[c, y, place]

    def produce(c):
        load_weight(c).wait()
        for place in range(SIDE):
            produce_block(c, place)

    def y_copy(c, step, part):
        yd = (y + step) % SIDE
        arrival = y_rsem.at[c] if part == ALL else first_rsem.at[c, (FAR, NEAR, OWN).index(part)]
        return pltpu.make_async_remote_copy(
            src_ref=ysend.at[c, yd, part], dst_ref=yrecv.at[c, part, y],
            send_sem=y_ssem, recv_sem=arrival,
            device_id=at_y(step), device_id_type=MESH,
        )

    def y_start(c, *parts):
        for part in parts:
            for step in (1, 2, 3):
                y_copy(c, step, part).start()

    def y_wait(c, part):
        arrival = y_rsem.at[c] if part == ALL else first_rsem.at[c, (FAR, NEAR, OWN).index(part)]
        drain(yrecv.at[c, part, slice(0, 3)], arrival)

    def table_copy(step):
        return pltpu.make_async_remote_copy(
            src_ref=table.at[z], dst_ref=table.at[z],
            send_sem=table_send, recv_sem=table_recv,
            device_id=at_z(step), device_id_type=MESH,
        )

    def far_copy(c, way):
        return pltpu.make_async_remote_copy(
            src_ref=far_send.at[c, way], dst_ref=far_recv.at[c, way],
            send_sem=far_ssem, recv_sem=far_rsem.at[c],
            device_id=at_z(1 if way == UP else 3), device_id_type=MESH,
        )

    def near_copy(c, way, part):
        lend = last & (lent == way)
        slot = jnp.where(lend, 1 - way, way)
        return pltpu.make_async_remote_copy(
            src_ref=near_send.at[c, way, part], dst_ref=near_recv.at[c, slot, part],
            send_sem=near_ssem, recv_sem=near_rsem.at[c, slot],
            device_id=at_z(1 if way == UP else 3, jnp.where(lend, twin, s)), device_id_type=MESH,
        )

    def near_wait(c, way):
        drain(near_recv.at[c, way], near_rsem.at[c, way])

    def twin_copy(c):
        return pltpu.make_async_remote_copy(
            src_ref=twin_send.at[c], dst_ref=twin_recv.at[c],
            send_sem=twin_ssem, recv_sem=twin_rsem.at[c],
            device_id=(twin, e), device_id_type=MESH,
        )

    def hand_copy(c):
        return pltpu.make_async_remote_copy(
            src_ref=layer.at[c], dst_ref=out_ref.at[:, columns(c)],
            send_sem=hand_ssem, recv_sem=hand_rsem,
            device_id=following, device_id_type=MESH,
        )

    def part_rows(part):
        return slice(part * half, (part + 1) * half)

    def partial(c, step, part):
        place = STEPS.index(step)
        mine = yrecv[c, place].reshape(group, CHUNK)
        return jnp.dot(mixing[place, part_rows(part)], mine, preferred_element_type=jnp.float32)

    def send_far(c):
        for way in (UP, DOWN):
            far_send[c, way] = partial(c, 2, 1 - way).astype(jnp.bfloat16)
            far_copy(c, way).start()

    def send_near(c):
        for way in (UP, DOWN):
            near_send[c, way, way] = partial(c, 1 if way == UP else 3, way).astype(jnp.bfloat16)
            near_copy(c, way, way).start()

    def pass_on(c):
        own = [partial(c, 1 if way == UP else 3, 1 - way) for way in (UP, DOWN)]
        drain(far_recv.at[c], far_rsem.at[c])
        for way in (UP, DOWN):
            near_send[c, way, 1 - way] = (own[way] + far_recv[c, way].astype(jnp.float32)).astype(jnp.bfloat16)
            near_copy(c, way, 1 - way).start()

    def finish(c):

        @pl.when(jnp.logical_not(last))
        def _():
            own = [partial(c, 0, part) for part in (0, 1)]
            near_wait(c, UP)
            near_wait(c, DOWN)
            for part in (0, 1):
                branch = own[part] + near_recv[c, UP, part].astype(jnp.float32) + near_recv[c, DOWN, part].astype(jnp.float32)
                branch = branch.astype(jnp.bfloat16).astype(jnp.float32)
                kept = residual[part_rows(part), columns(c)].astype(jnp.float32)
                layer[c, part_rows(part)] = (kept + branch).astype(jnp.bfloat16)
            hand_copy(c).start()

        for way, here in ((UP, s < RUN), (DOWN, s >= RUN)):
            @pl.when(last & here)
            def _():
                own = [partial(c, 0, part) for part in (0, 1)]
                near_wait(c, way)
                for part in (0, 1):
                    branch = own[part] + near_recv[c, way, part].astype(jnp.float32)
                    kept = residual[part_rows(part), columns(c)].astype(jnp.float32)
                    twin_send[c, part_rows(part)] = (kept + branch).astype(jnp.bfloat16)
                twin_copy(c).start()

    def finish_twin(c):
        for way, here in ((DOWN, s < RUN), (UP, s >= RUN)):
            @pl.when(here)
            def _():
                twin_copy(c).wait_recv()
                near_wait(c, way)
                for part in (0, 1):
                    summed = twin_recv[c, part_rows(part)].astype(jnp.float32) + near_recv[c, way, part].astype(jnp.float32)
                    layer[c, part_rows(part)] = summed.astype(jnp.bfloat16)
        hand_copy(c).start()

    def mix(place):
        entry = table[(z + STEPS[place]) % SIDE]
        slot = lax.broadcasted_iota(jnp.int32, (group, rows), 0).astype(jnp.float32) + (z * group).astype(jnp.float32)
        weights = jnp.where(slot == entry[0:1], entry[2:3], 0.0) + jnp.where(slot == entry[1:2], entry[3:4], 0.0)
        mixing[place] = weights.T.astype(jnp.bfloat16)

    load_hidden(0).wait()
    load_weight(0).wait()
    produce_block(0, 0)
    pl.semaphore_wait(barrier, len(partners) + jnp.where(last, 2, 0))
    for step in (1, 2, 3):
        table_copy(step).start()
    y_start(0, FAR)
    for c in range(1, READ):
        load_weight(c).start()
    for place in (1, 2, 3):
        load_hidden(place).wait()
        produce_block(0, place)
        if place == 2:
            y_start(0, NEAR)
    y_start(0, OWN)
    drain(table.at[0:3], table_recv)
    def parts(c):
        return (FAR, NEAR, OWN) if isinstance(c, int) and c < SPLIT else (ALL,)

    mix(0)
    y_wait(0, FAR)
    send_far(0)
    produce(1)
    y_start(1, *parts(1))
    for place in (1, 2, 3):
        mix(place)
    load_residual.start()

    def turn(i):
        @pl.when(i < chunks - AHEAD - 1)
        def _():
            y_start(i + AHEAD + 1, *parts(i + AHEAD + 1))

        @pl.when(i < chunks - READ)
        def _():
            load_weight(i + READ).start()

        @pl.when(i < chunks)
        def _():
            for part in parts(i)[1:]:
                y_wait(i, part)
            send_near(i)

        @pl.when((i >= 1) & (i <= chunks))
        def _():
            pass_on(i - 1)

        @pl.when(i < chunks - 1)
        def _():
            y_wait(i + 1, parts(i + 1)[0])
            send_far(i + 1)

        @pl.when(i < chunks - AHEAD - 2)
        def _():
            produce(i + AHEAD + 2)

        @pl.when((i >= 2) & (i < chunks + 2))
        def _():
            finish(i - 2)

        @pl.when(last & (i >= 3))
        def _():
            finish_twin(i - 3)

    for c in range(2, AHEAD + 2):
        produce(c)
        if c <= AHEAD:
            y_start(c, *parts(c))
    for i in range(2):
        turn(i)
    load_residual.wait()
    for i in range(2, SPLIT):
        turn(i)
    pl.loop(SPLIT, chunks + 3)(turn)

    drain(table.at[0:3], table_send)
    drain(ysend.at[:, 0:3], y_ssem)
    drain(far_send, far_ssem)
    drain(near_send, near_ssem)

    @pl.when(last)
    def _():
        drain(twin_send, twin_ssem)

    drain(layer, hand_ssem)
    drain(layer, hand_rsem)


def local(hidden, down_weight, expert_ids, route_gates, residual):
    sections = lax.axis_size("section")
    slots, depth = hidden.shape[2:]
    rows, width = residual.shape
    cap = slots // (SIDE * SIDE)
    chunks = width // CHUNK
    group = SIDE * cap
    bf16, f32 = jnp.bfloat16, jnp.float32
    in_hbm = pl.BlockSpec(memory_space=pltpu.HBM)
    vmem = pl.BlockSpec(memory_space=pltpu.VMEM)
    dma = pltpu.SemaphoreType.DMA
    return pl.pallas_call(
        functools.partial(kernel, sections, chunks, cap),
        out_shape=pltpu.VMEM((rows, width), bf16),
        in_specs=[in_hbm, in_hbm, vmem, vmem, in_hbm],
        out_specs=vmem,
        scratch_shapes=[
            pltpu.VMEM((SIDE, group, depth), bf16),
            pltpu.VMEM((chunks, depth, CHUNK), bf16),
            pltpu.VMEM((rows, width), bf16),
            pltpu.VMEM((chunks, SIDE, SIDE, cap, CHUNK), bf16),
            pltpu.VMEM((chunks, SIDE, SIDE, cap, CHUNK), bf16),
            pltpu.VMEM((chunks, 2, rows // 2, CHUNK), bf16),
            pltpu.VMEM((chunks, 2, rows // 2, CHUNK), bf16),
            pltpu.VMEM((chunks, 2, 2, rows // 2, CHUNK), bf16),
            pltpu.VMEM((chunks, 2, 2, rows // 2, CHUNK), bf16),
            pltpu.VMEM((chunks, rows, CHUNK), bf16),
            pltpu.VMEM((chunks, rows, CHUNK), bf16),
            pltpu.VMEM((chunks, rows, CHUNK), bf16),
            pltpu.VMEM((SIDE, 8, rows), f32),
            pltpu.VMEM((SIDE, rows, group), bf16),
            dma((SIDE,)), dma((chunks,)), dma(()), dma(()), dma(()),
            dma(()), dma((SPLIT, 3)), dma((chunks,)),
            dma(()), dma((chunks,)),
            dma(()), dma((chunks, 2)),
            dma(()), dma((chunks,)),
            dma(()), dma(()),
        ],
        compiler_params=pltpu.CompilerParams(
            collective_id=0, has_side_effects=True, vmem_limit_bytes=61 * 2**20
        ),
        cost_estimate=pl.CostEstimate(
            flops=2 * slots * width * (depth + rows), bytes_accessed=2 * (slots * depth + depth * width + 2 * rows * width),
            transcendentals=0,
        ),
        name="down_combine_handoff",
    )(hidden, down_weight, expert_ids.T, route_gates.T, residual)


def solution(mesh):
    return jax.shard_map(
        local,
        mesh=mesh,
        in_specs=(
            P("section", "expert", None, None),
            P("section", "expert", None, None),
            P(("section", "expert"), None),
            P(("section", "expert"), None),
            P(("section", "expert"), None),
        ),
        out_specs=P(("section", "expert"), None),
        check_vma=False,
    )
```

```python
import functools

import jax
import jax.numpy as jnp
from jax import lax
from jax.experimental import pallas as pl
from jax.experimental.pallas import tpu as pltpu
from jax.sharding import PartitionSpec as P

MESH = pl.DeviceIdType.MESH
SIDE = 4
RUN = 8
CHUNK = 256
READ = 5
SPLIT = 2
AHEAD = 1
STEPS = (2, 1, 3, 0)
FAR, NEAR, OWN = slice(0, 1), slice(1, 3), slice(3, 4)
ALL = slice(0, 4)
LAG = 2
UP, DOWN = 0, 1


def kernel(
    sections, chunks, cap,
    hidden_hbm, weight_hbm, ids_ref, gates_ref, residual_hbm,
    out_ref,
    hidden, weight, residual, ysend, yrecv, far_send, far_recv, near_send, near_recv, twin_send, twin_recv, layer,
    table, mixing,
    hidden_sem, weight_sem, residual_sem, table_send, table_recv,
    y_ssem, first_rsem, y_rsem, far_ssem, far_rsem, near_ssem, near_rsem, twin_ssem, twin_rsem, hand_ssem, hand_rsem,
):
    s, e = lax.axis_index("section"), lax.axis_index("expert")
    z, y = e // SIDE, e % SIDE
    group = SIDE * cap
    rows = ids_ref.shape[1]
    half = rows // 2

    def at_y(step):
        return (s, z * SIDE + (y + step) % SIDE)

    def at_z(step, section=s):
        return (section, ((z + step) % SIDE) * SIDE + y)

    last = s % RUN == RUN - 1
    twin = (s + RUN) % sections
    lent = jnp.where(s < RUN, DOWN, UP)
    following = (jnp.where(last, (twin + 1) % sections, (s + 1) % sections), e)
    preceding = (jnp.where(s % RUN == 0, (s + RUN - 1) % sections, (s + sections - 1) % sections), e)
    lender = at_z(jnp.where(s < RUN, SIDE - 1, 1), twin)

    barrier = pltpu.get_barrier_semaphore()
    partners = [at_y(1), at_y(2), at_y(3), at_z(1), at_z(2), at_z(3), preceding]
    for partner in partners:
        pl.semaphore_signal(barrier, inc=1, device_id=partner, device_id_type=MESH)

    @pl.when(last)
    def _():
        for partner in (lender, (twin, e)):
            pl.semaphore_signal(barrier, inc=1, device_id=partner, device_id_type=MESH)

    def columns(c):
        return pl.ds(pl.multiple_of(c * CHUNK, CHUNK), CHUNK)

    def load_weight(c):
        return pltpu.make_async_copy(weight_hbm.at[0, 0, :, columns(c)], weight.at[c], weight_sem.at[c])

    load_residual = pltpu.make_async_copy(residual_hbm, residual, residual_sem)

    def drain(ref, sem):
        pltpu.make_async_copy(ref, ref, sem).wait()

    def load_hidden(place):
        block = pl.ds(pl.multiple_of(((z + STEPS[place]) % SIDE) * group, group), group)
        return pltpu.make_async_copy(hidden_hbm.at[0, 0, block], hidden.at[place], hidden_sem.at[place])

    load_hidden(0).start()
    load_weight(0).start()
    for place in (1, 2, 3):
        load_hidden(place).start()

    ids = ids_ref[...]
    experts = lax.broadcasted_iota(jnp.int32, (SIDE * SIDE, rows), 0)
    named = [(experts == ids[k:k + 1]).astype(jnp.float32) for k in range(2)]
    earlier = (lax.broadcasted_iota(jnp.int32, (rows, rows), 0) < lax.broadcasted_iota(jnp.int32, (rows, rows), 1))
    before = jnp.dot(
        (named[0] + named[1]).astype(jnp.bfloat16), earlier.astype(jnp.bfloat16), preferred_element_type=jnp.float32
    )
    slots = [
        ids[k:k + 1].astype(jnp.float32) * cap + jnp.sum(before * named[k], axis=0, keepdims=True) for k in range(2)
    ]
    gates = gates_ref[...].astype(jnp.float32)
    table[z] = jnp.concatenate([slots[0], slots[1], gates, jnp.zeros((4, rows), jnp.float32)], axis=0)

    def produce_block(c, place):
        block = jnp.dot(hidden[place], weight[c], preferred_element_type=jnp.float32).astype(jnp.bfloat16)
        ysend[c, :, place] = block.reshape(SIDE, cap, CHUNK)
        yrecv[c, place, y] = ysend[c, y, place]

    def produce(c):
        load_weight(c).wait()
        for place in range(SIDE):
            produce_block(c, place)

    def y_copy(c, step, part):
        yd = (y + step) % SIDE
        arrival = y_rsem.at[c] if part == ALL else first_rsem.at[c, (FAR, NEAR, OWN).index(part)]
        return pltpu.make_async_remote_copy(
            src_ref=ysend.at[c, yd, part], dst_ref=yrecv.at[c, part, y],
            send_sem=y_ssem, recv_sem=arrival,
            device_id=at_y(step), device_id_type=MESH,
        )

    def y_start(c, *parts):
        for part in parts:
            for step in (1, 2, 3):
                y_copy(c, step, part).start()

    def y_wait(c, part):
        arrival = y_rsem.at[c] if part == ALL else first_rsem.at[c, (FAR, NEAR, OWN).index(part)]
        drain(yrecv.at[c, part, slice(0, 3)], arrival)

    def table_copy(step):
        return pltpu.make_async_remote_copy(
            src_ref=table.at[z], dst_ref=table.at[z],
            send_sem=table_send, recv_sem=table_recv,
            device_id=at_z(step), device_id_type=MESH,
        )

    def far_copy(c, way):
        return pltpu.make_async_remote_copy(
            src_ref=far_send.at[c, way], dst_ref=far_recv.at[c, way],
            send_sem=far_ssem, recv_sem=far_rsem.at[c],
            device_id=at_z(1 if way == UP else 3), device_id_type=MESH,
        )

    def near_copy(c, way, part):
        lend = last & (lent == way)
        slot = jnp.where(lend, 1 - way, way)
        return pltpu.make_async_remote_copy(
            src_ref=near_send.at[c, way, part], dst_ref=near_recv.at[c, slot, part],
            send_sem=near_ssem, recv_sem=near_rsem.at[c, slot],
            device_id=at_z(1 if way == UP else 3, jnp.where(lend, twin, s)), device_id_type=MESH,
        )

    def near_wait(c, way):
        drain(near_recv.at[c, way], near_rsem.at[c, way])

    def twin_copy(c):
        return pltpu.make_async_remote_copy(
            src_ref=twin_send.at[c], dst_ref=twin_recv.at[c],
            send_sem=twin_ssem, recv_sem=twin_rsem.at[c],
            device_id=(twin, e), device_id_type=MESH,
        )

    def part_rows(part):
        return slice(part * half, (part + 1) * half)

    def hand_copy(c, part):
        return pltpu.make_async_remote_copy(
            src_ref=layer.at[c, part_rows(part)], dst_ref=out_ref.at[part_rows(part), columns(c)],
            send_sem=hand_ssem, recv_sem=hand_rsem,
            device_id=following, device_id_type=MESH,
        )

    def partial(c, step, part):
        place = STEPS.index(step)
        mine = yrecv[c, place].reshape(group, CHUNK)
        return jnp.dot(mixing[place, part_rows(part)], mine, preferred_element_type=jnp.float32)

    def send_far(c):
        for way in (UP, DOWN):
            far_send[c, way] = partial(c, 2, 1 - way).astype(jnp.bfloat16)
            far_copy(c, way).start()

    def send_near(c):
        for way in (UP, DOWN):
            near_send[c, way, way] = partial(c, 1 if way == UP else 3, way).astype(jnp.bfloat16)
            near_copy(c, way, way).start()

    def pass_on(c):
        own = [partial(c, 1 if way == UP else 3, 1 - way) for way in (UP, DOWN)]
        drain(far_recv.at[c], far_rsem.at[c])
        for way in (UP, DOWN):
            near_send[c, way, 1 - way] = (own[way] + far_recv[c, way].astype(jnp.float32)).astype(jnp.bfloat16)
            near_copy(c, way, 1 - way).start()

    def finish(c):

        @pl.when(jnp.logical_not(last))
        def _():
            own = [partial(c, 0, part) for part in (0, 1)]
            near_wait(c, UP)
            near_wait(c, DOWN)
            for part in (0, 1):
                branch = own[part] + near_recv[c, UP, part].astype(jnp.float32) + near_recv[c, DOWN, part].astype(jnp.float32)
                branch = branch.astype(jnp.bfloat16).astype(jnp.float32)
                kept = residual[part_rows(part), columns(c)].astype(jnp.float32)
                layer[c, part_rows(part)] = (kept + branch).astype(jnp.bfloat16)
                hand_copy(c, part).start()

        for way, here in ((UP, s < RUN), (DOWN, s >= RUN)):
            @pl.when(last & here)
            def _():
                own = [partial(c, 0, part) for part in (0, 1)]
                near_wait(c, way)
                for part in (0, 1):
                    branch = own[part] + near_recv[c, way, part].astype(jnp.float32)
                    kept = residual[part_rows(part), columns(c)].astype(jnp.float32)
                    twin_send[c, part_rows(part)] = (kept + branch).astype(jnp.bfloat16)
                twin_copy(c).start()

    def finish_twin(c):
        for way, here in ((DOWN, s < RUN), (UP, s >= RUN)):
            @pl.when(here)
            def _():
                twin_copy(c).wait_recv()
                near_wait(c, way)
                for part in (0, 1):
                    summed = twin_recv[c, part_rows(part)].astype(jnp.float32) + near_recv[c, way, part].astype(jnp.float32)
                    layer[c, part_rows(part)] = summed.astype(jnp.bfloat16)
                    hand_copy(c, part).start()

    def mix(place):
        entry = table[(z + STEPS[place]) % SIDE]
        slot = lax.broadcasted_iota(jnp.int32, (group, rows), 0).astype(jnp.float32) + (z * group).astype(jnp.float32)
        weights = jnp.where(slot == entry[0:1], entry[2:3], 0.0) + jnp.where(slot == entry[1:2], entry[3:4], 0.0)
        mixing[place] = weights.T.astype(jnp.bfloat16)

    load_hidden(0).wait()
    load_weight(0).wait()
    produce_block(0, 0)
    pl.semaphore_wait(barrier, len(partners) + jnp.where(last, 2, 0))
    for step in (1, 2, 3):
        table_copy(step).start()
    y_start(0, FAR)
    for c in range(1, READ):
        load_weight(c).start()
    for place in (1, 2, 3):
        load_hidden(place).wait()
        produce_block(0, place)
        if place == 2:
            y_start(0, NEAR)
    y_start(0, OWN)
    drain(table.at[0:3], table_recv)
    def parts(c):
        return (FAR, NEAR, OWN) if isinstance(c, int) and c < SPLIT else (ALL,)

    mix(0)
    y_wait(0, FAR)
    send_far(0)
    produce(1)
    y_start(1, *parts(1))
    for place in (1, 2, 3):
        mix(place)
    load_residual.start()

    def turn(i):
        @pl.when(i < chunks - AHEAD - 1)
        def _():
            y_start(i + AHEAD + 1, *parts(i + AHEAD + 1))

        @pl.when(i < chunks - READ)
        def _():
            load_weight(i + READ).start()

        @pl.when(i < chunks)
        def _():
            for part in parts(i)[1:]:
                y_wait(i, part)
            send_near(i)

        @pl.when((i >= 1) & (i <= chunks))
        def _():
            pass_on(i - 1)

        @pl.when(i < chunks - 1)
        def _():
            y_wait(i + 1, parts(i + 1)[0])
            send_far(i + 1)

        @pl.when(i < chunks - AHEAD - 2)
        def _():
            produce(i + AHEAD + 2)

        @pl.when((i >= LAG) & (i < chunks + LAG))
        def _():
            finish(i - LAG)

        @pl.when(last & (i > LAG))
        def _():
            finish_twin(i - LAG - 1)

    for c in range(2, AHEAD + 2):
        produce(c)
        if c <= AHEAD:
            y_start(c, *parts(c))
    for i in range(2):
        turn(i)
    load_residual.wait()
    for i in range(2, SPLIT):
        turn(i)
    pl.loop(SPLIT, chunks + LAG + 1)(turn)

    drain(table.at[0:3], table_send)
    drain(ysend.at[:, 0:3], y_ssem)
    drain(far_send, far_ssem)
    drain(near_send, near_ssem)

    @pl.when(last)
    def _():
        drain(twin_send, twin_ssem)

    drain(layer, hand_ssem)
    drain(layer, hand_rsem)


def local(hidden, down_weight, expert_ids, route_gates, residual):
    sections = lax.axis_size("section")
    slots, depth = hidden.shape[2:]
    rows, width = residual.shape
    cap = slots // (SIDE * SIDE)
    chunks = width // CHUNK
    group = SIDE * cap
    bf16, f32 = jnp.bfloat16, jnp.float32
    in_hbm = pl.BlockSpec(memory_space=pltpu.HBM)
    vmem = pl.BlockSpec(memory_space=pltpu.VMEM)
    dma = pltpu.SemaphoreType.DMA
    return pl.pallas_call(
        functools.partial(kernel, sections, chunks, cap),
        out_shape=pltpu.VMEM((rows, width), bf16),
        in_specs=[in_hbm, in_hbm, vmem, vmem, in_hbm],
        out_specs=vmem,
        scratch_shapes=[
            pltpu.VMEM((SIDE, group, depth), bf16),
            pltpu.VMEM((chunks, depth, CHUNK), bf16),
            pltpu.VMEM((rows, width), bf16),
            pltpu.VMEM((chunks, SIDE, SIDE, cap, CHUNK), bf16),
            pltpu.VMEM((chunks, SIDE, SIDE, cap, CHUNK), bf16),
            pltpu.VMEM((chunks, 2, rows // 2, CHUNK), bf16),
            pltpu.VMEM((chunks, 2, rows // 2, CHUNK), bf16),
            pltpu.VMEM((chunks, 2, 2, rows // 2, CHUNK), bf16),
            pltpu.VMEM((chunks, 2, 2, rows // 2, CHUNK), bf16),
            pltpu.VMEM((chunks, rows, CHUNK), bf16),
            pltpu.VMEM((chunks, rows, CHUNK), bf16),
            pltpu.VMEM((chunks, rows, CHUNK), bf16),
            pltpu.VMEM((SIDE, 8, rows), f32),
            pltpu.VMEM((SIDE, rows, group), bf16),
            dma((SIDE,)), dma((chunks,)), dma(()), dma(()), dma(()),
            dma(()), dma((SPLIT, 3)), dma((chunks,)),
            dma(()), dma((chunks,)),
            dma(()), dma((chunks, 2)),
            dma(()), dma((chunks,)),
            dma(()), dma(()),
        ],
        compiler_params=pltpu.CompilerParams(
            collective_id=0, has_side_effects=True, vmem_limit_bytes=61 * 2**20
        ),
        cost_estimate=pl.CostEstimate(
            flops=2 * slots * width * (depth + rows), bytes_accessed=2 * (slots * depth + depth * width + 2 * rows * width),
            transcendentals=0,
        ),
        name="down_combine_handoff",
    )(hidden, down_weight, expert_ids.T, route_gates.T, residual)


def solution(mesh):
    return jax.shard_map(
        local,
        mesh=mesh,
        in_specs=(
            P("section", "expert", None, None),
            P("section", "expert", None, None),
            P(("section", "expert"), None),
            P(("section", "expert"), None),
            P(("section", "expert"), None),
        ),
        out_specs=P(("section", "expert"), None),
        check_vma=False,
    )
```

```python
import functools

import jax
import jax.numpy as jnp
from jax import lax
from jax.experimental import pallas as pl
from jax.experimental.pallas import tpu as pltpu
from jax.sharding import PartitionSpec as P

MESH = pl.DeviceIdType.MESH
SIDE = 4
RUN = 8
CHUNK = 256
READ = 5
SPLIT = 2
AHEAD = 1
STEPS = (2, 1, 3, 0)
FAR, NEAR, OWN = slice(0, 1), slice(1, 3), slice(3, 4)
ALL = slice(0, 4)
RING = 4
UP, DOWN = 0, 1


def kernel(
    sections, chunks, cap,
    hidden_hbm, weight_hbm, ids_ref, gates_ref, residual_hbm,
    out_ref,
    hidden, weight, residual, ysend, yrecv, far_send, far_recv, near_send, near_recv, twin_send, twin_recv, layer,
    table, mixing,
    hidden_sem, weight_sem, residual_sem, table_send, table_recv,
    y_ssem, first_rsem, y_rsem, far_ssem, far_rsem, near_ssem, near_rsem, twin_ssem, twin_rsem, hand_ssem, hand_rsem,
):
    s, e = lax.axis_index("section"), lax.axis_index("expert")
    z, y = e // SIDE, e % SIDE
    group = SIDE * cap
    rows = ids_ref.shape[1]
    half = rows // 2

    def at_y(step):
        return (s, z * SIDE + (y + step) % SIDE)

    def at_z(step, section=s):
        return (section, ((z + step) % SIDE) * SIDE + y)

    last = s % RUN == RUN - 1
    twin = (s + RUN) % sections
    lent = jnp.where(s < RUN, DOWN, UP)
    following = (jnp.where(last, (twin + 1) % sections, (s + 1) % sections), e)
    preceding = (jnp.where(s % RUN == 0, (s + RUN - 1) % sections, (s + sections - 1) % sections), e)
    lender = at_z(jnp.where(s < RUN, SIDE - 1, 1), twin)

    barrier = pltpu.get_barrier_semaphore()
    partners = [at_y(1), at_y(2), at_y(3), at_z(1), at_z(2), at_z(3), preceding]
    for partner in partners:
        pl.semaphore_signal(barrier, inc=1, device_id=partner, device_id_type=MESH)

    @pl.when(last)
    def _():
        for partner in (lender, (twin, e)):
            pl.semaphore_signal(barrier, inc=1, device_id=partner, device_id_type=MESH)

    def columns(c):
        return pl.ds(pl.multiple_of(c * CHUNK, CHUNK), CHUNK)

    def load_weight(c):
        return pltpu.make_async_copy(weight_hbm.at[0, 0, :, columns(c)], weight.at[c], weight_sem.at[c % (2 * RING)])

    load_residual = pltpu.make_async_copy(residual_hbm, residual, residual_sem)

    def drain(ref, sem):
        pltpu.make_async_copy(ref, ref, sem).wait()

    def load_hidden(place):
        block = pl.ds(pl.multiple_of(((z + STEPS[place]) % SIDE) * group, group), group)
        return pltpu.make_async_copy(hidden_hbm.at[0, 0, block], hidden.at[place], hidden_sem.at[place])

    load_hidden(0).start()
    load_weight(0).start()
    for place in (1, 2, 3):
        load_hidden(place).start()

    ids = ids_ref[...]
    experts = lax.broadcasted_iota(jnp.int32, (SIDE * SIDE, rows), 0)
    named = [(experts == ids[k:k + 1]).astype(jnp.float32) for k in range(2)]
    earlier = (lax.broadcasted_iota(jnp.int32, (rows, rows), 0) < lax.broadcasted_iota(jnp.int32, (rows, rows), 1))
    before = jnp.dot(
        (named[0] + named[1]).astype(jnp.bfloat16), earlier.astype(jnp.bfloat16), preferred_element_type=jnp.float32
    )
    slots = [
        ids[k:k + 1].astype(jnp.float32) * cap + jnp.sum(before * named[k], axis=0, keepdims=True) for k in range(2)
    ]
    gates = gates_ref[...].astype(jnp.float32)
    table[z] = jnp.concatenate([slots[0], slots[1], gates, jnp.zeros((4, rows), jnp.float32)], axis=0)

    def produce_block(c, place):
        block = jnp.dot(hidden[place], weight[c], preferred_element_type=jnp.float32).astype(jnp.bfloat16)
        ysend[c, :, place] = block.reshape(SIDE, cap, CHUNK)
        yrecv[c, place, y] = ysend[c, y, place]

    def produce(c):
        load_weight(c).wait()
        for place in range(SIDE):
            produce_block(c, place)

    def y_copy(c, step, part):
        yd = (y + step) % SIDE
        arrival = y_rsem.at[c % RING] if part == ALL else first_rsem.at[c, (FAR, NEAR, OWN).index(part)]
        return pltpu.make_async_remote_copy(
            src_ref=ysend.at[c, yd, part], dst_ref=yrecv.at[c, part, y],
            send_sem=y_ssem, recv_sem=arrival,
            device_id=at_y(step), device_id_type=MESH,
        )

    def y_start(c, *parts):
        for part in parts:
            for step in (1, 2, 3):
                y_copy(c, step, part).start()

    def y_wait(c, part):
        arrival = y_rsem.at[c % RING] if part == ALL else first_rsem.at[c, (FAR, NEAR, OWN).index(part)]
        drain(yrecv.at[c, part, slice(0, 3)], arrival)

    def table_copy(step):
        return pltpu.make_async_remote_copy(
            src_ref=table.at[z], dst_ref=table.at[z],
            send_sem=table_send, recv_sem=table_recv,
            device_id=at_z(step), device_id_type=MESH,
        )

    def far_copy(c, way):
        return pltpu.make_async_remote_copy(
            src_ref=far_send.at[c, way], dst_ref=far_recv.at[c, way],
            send_sem=far_ssem, recv_sem=far_rsem.at[c % RING],
            device_id=at_z(1 if way == UP else 3), device_id_type=MESH,
        )

    def near_copy(c, way, part):
        lend = last & (lent == way)
        slot = jnp.where(lend, 1 - way, way)
        return pltpu.make_async_remote_copy(
            src_ref=near_send.at[c, way, part], dst_ref=near_recv.at[c, slot, part],
            send_sem=near_ssem, recv_sem=near_rsem.at[c % (2 * RING), slot],
            device_id=at_z(1 if way == UP else 3, jnp.where(lend, twin, s)), device_id_type=MESH,
        )

    def near_wait(c, way):
        drain(near_recv.at[c, way], near_rsem.at[c % (2 * RING), way])

    def twin_copy(c):
        return pltpu.make_async_remote_copy(
            src_ref=twin_send.at[c], dst_ref=twin_recv.at[c],
            send_sem=twin_ssem, recv_sem=twin_rsem.at[c % RING],
            device_id=(twin, e), device_id_type=MESH,
        )

    def hand_copy(c):
        return pltpu.make_async_remote_copy(
            src_ref=layer.at[c], dst_ref=out_ref.at[:, columns(c)],
            send_sem=hand_ssem, recv_sem=hand_rsem,
            device_id=following, device_id_type=MESH,
        )

    def part_rows(part):
        return slice(part * half, (part + 1) * half)

    def partial(c, step, part):
        place = STEPS.index(step)
        mine = yrecv[c, place].reshape(group, CHUNK)
        return jnp.dot(mixing[place, part_rows(part)], mine, preferred_element_type=jnp.float32)

    def send_far(c):
        for way in (UP, DOWN):
            far_send[c, way] = partial(c, 2, 1 - way).astype(jnp.bfloat16)
            far_copy(c, way).start()

    def send_near(c):
        for way in (UP, DOWN):
            near_send[c, way, way] = partial(c, 1 if way == UP else 3, way).astype(jnp.bfloat16)
            near_copy(c, way, way).start()

    def pass_on(c):
        own = [partial(c, 1 if way == UP else 3, 1 - way) for way in (UP, DOWN)]
        drain(far_recv.at[c], far_rsem.at[c % RING])
        for way in (UP, DOWN):
            near_send[c, way, 1 - way] = (own[way] + far_recv[c, way].astype(jnp.float32)).astype(jnp.bfloat16)
            near_copy(c, way, 1 - way).start()

    def finish(c):

        @pl.when(jnp.logical_not(last))
        def _():
            own = [partial(c, 0, part) for part in (0, 1)]
            near_wait(c, UP)
            near_wait(c, DOWN)
            for part in (0, 1):
                branch = own[part] + near_recv[c, UP, part].astype(jnp.float32) + near_recv[c, DOWN, part].astype(jnp.float32)
                branch = branch.astype(jnp.bfloat16).astype(jnp.float32)
                kept = residual[part_rows(part), columns(c)].astype(jnp.float32)
                layer[c, part_rows(part)] = (kept + branch).astype(jnp.bfloat16)
            hand_copy(c).start()

        for way, here in ((UP, s < RUN), (DOWN, s >= RUN)):
            @pl.when(last & here)
            def _():
                own = [partial(c, 0, part) for part in (0, 1)]
                near_wait(c, way)
                for part in (0, 1):
                    branch = own[part] + near_recv[c, way, part].astype(jnp.float32)
                    kept = residual[part_rows(part), columns(c)].astype(jnp.float32)
                    twin_send[c, part_rows(part)] = (kept + branch).astype(jnp.bfloat16)
                twin_copy(c).start()

    def finish_twin(c):
        for way, here in ((DOWN, s < RUN), (UP, s >= RUN)):
            @pl.when(here)
            def _():
                twin_copy(c).wait_recv()
                near_wait(c, way)
                for part in (0, 1):
                    summed = twin_recv[c, part_rows(part)].astype(jnp.float32) + near_recv[c, way, part].astype(jnp.float32)
                    layer[c, part_rows(part)] = summed.astype(jnp.bfloat16)
        hand_copy(c).start()

    def mix(place):
        entry = table[(z + STEPS[place]) % SIDE]
        slot = lax.broadcasted_iota(jnp.int32, (group, rows), 0).astype(jnp.float32) + (z * group).astype(jnp.float32)
        weights = jnp.where(slot == entry[0:1], entry[2:3], 0.0) + jnp.where(slot == entry[1:2], entry[3:4], 0.0)
        mixing[place] = weights.T.astype(jnp.bfloat16)

    load_hidden(0).wait()
    load_weight(0).wait()
    produce_block(0, 0)
    pl.semaphore_wait(barrier, len(partners) + jnp.where(last, 2, 0))
    for step in (1, 2, 3):
        table_copy(step).start()
    y_start(0, FAR)
    for c in range(1, READ):
        load_weight(c).start()
    for place in (1, 2, 3):
        load_hidden(place).wait()
        produce_block(0, place)
        if place == 2:
            y_start(0, NEAR)
    y_start(0, OWN)
    drain(table.at[0:3], table_recv)
    def parts(c):
        return (FAR, NEAR, OWN) if isinstance(c, int) and c < SPLIT else (ALL,)

    mix(0)
    y_wait(0, FAR)
    send_far(0)
    produce(1)
    y_start(1, *parts(1))
    for place in (1, 2, 3):
        mix(place)
    load_residual.start()

    def turn(i):
        @pl.when(i < chunks - AHEAD - 1)
        def _():
            y_start(i + AHEAD + 1, *parts(i + AHEAD + 1))

        @pl.when(i < chunks - READ)
        def _():
            load_weight(i + READ).start()

        @pl.when(i < chunks)
        def _():
            for part in parts(i)[1:]:
                y_wait(i, part)
            send_near(i)

        @pl.when((i >= 1) & (i <= chunks))
        def _():
            pass_on(i - 1)

        @pl.when(i < chunks - 1)
        def _():
            y_wait(i + 1, parts(i + 1)[0])
            send_far(i + 1)

        @pl.when(i < chunks - AHEAD - 2)
        def _():
            produce(i + AHEAD + 2)

        @pl.when((i >= 2) & (i < chunks + 2))
        def _():
            finish(i - 2)

        @pl.when(last & (i >= 3))
        def _():
            finish_twin(i - 3)

    for c in range(2, AHEAD + 2):
        produce(c)
        if c <= AHEAD:
            y_start(c, *parts(c))
    for i in range(2):
        turn(i)
    load_residual.wait()
    for i in range(2, SPLIT):
        turn(i)
    pl.loop(SPLIT, chunks + 3)(turn)

    drain(table.at[0:3], table_send)
    drain(ysend.at[:, 0:3], y_ssem)
    drain(far_send, far_ssem)
    drain(near_send, near_ssem)

    @pl.when(last)
    def _():
        drain(twin_send, twin_ssem)

    drain(layer, hand_ssem)
    drain(layer, hand_rsem)


def local(hidden, down_weight, expert_ids, route_gates, residual):
    sections = lax.axis_size("section")
    slots, depth = hidden.shape[2:]
    rows, width = residual.shape
    cap = slots // (SIDE * SIDE)
    chunks = width // CHUNK
    group = SIDE * cap
    bf16, f32 = jnp.bfloat16, jnp.float32
    in_hbm = pl.BlockSpec(memory_space=pltpu.HBM)
    vmem = pl.BlockSpec(memory_space=pltpu.VMEM)
    dma = pltpu.SemaphoreType.DMA
    return pl.pallas_call(
        functools.partial(kernel, sections, chunks, cap),
        out_shape=pltpu.VMEM((rows, width), bf16),
        in_specs=[in_hbm, in_hbm, vmem, vmem, in_hbm],
        out_specs=vmem,
        scratch_shapes=[
            pltpu.VMEM((SIDE, group, depth), bf16),
            pltpu.VMEM((chunks, depth, CHUNK), bf16),
            pltpu.VMEM((rows, width), bf16),
            pltpu.VMEM((chunks, SIDE, SIDE, cap, CHUNK), bf16),
            pltpu.VMEM((chunks, SIDE, SIDE, cap, CHUNK), bf16),
            pltpu.VMEM((chunks, 2, rows // 2, CHUNK), bf16),
            pltpu.VMEM((chunks, 2, rows // 2, CHUNK), bf16),
            pltpu.VMEM((chunks, 2, 2, rows // 2, CHUNK), bf16),
            pltpu.VMEM((chunks, 2, 2, rows // 2, CHUNK), bf16),
            pltpu.VMEM((chunks, rows, CHUNK), bf16),
            pltpu.VMEM((chunks, rows, CHUNK), bf16),
            pltpu.VMEM((chunks, rows, CHUNK), bf16),
            pltpu.VMEM((SIDE, 8, rows), f32),
            pltpu.VMEM((SIDE, rows, group), bf16),
            dma((SIDE,)), dma((2 * RING,)), dma(()), dma(()), dma(()),
            dma(()), dma((SPLIT, 3)), dma((RING,)),
            dma(()), dma((RING,)),
            dma(()), dma((2 * RING, 2)),
            dma(()), dma((RING,)),
            dma(()), dma(()),
        ],
        compiler_params=pltpu.CompilerParams(
            collective_id=0, has_side_effects=True, vmem_limit_bytes=61 * 2**20
        ),
        cost_estimate=pl.CostEstimate(
            flops=2 * slots * width * (depth + rows), bytes_accessed=2 * (slots * depth + depth * width + 2 * rows * width),
            transcendentals=0,
        ),
        name="down_combine_handoff",
    )(hidden, down_weight, expert_ids.T, route_gates.T, residual)


def solution(mesh):
    return jax.shard_map(
        local,
        mesh=mesh,
        in_specs=(
            P("section", "expert", None, None),
            P("section", "expert", None, None),
            P(("section", "expert"), None),
            P(("section", "expert"), None),
            P(("section", "expert"), None),
        ),
        out_specs=P(("section", "expert"), None),
        check_vma=False,
    )
```
